256 devices in a mesh: rep: 32 (over z_lo, x, core), tp: 8 (over z_hi, y).
Axes of the slice: x: 4, y: 4, z: 8 (z_hi: 2, z_lo: 4; z = z_hi * 4 + z_lo), core: 2. Of those that a mesh axis runs over, the one named last changes fastest.
Arguments:
- tokens: bfloat16 [16384, 8192], P('rep'), may hold values from -6 to 6
- w_query: bfloat16 [8192, 4096], P('rep', 'tp'), may hold values from -1 to 1
- w_key: bfloat16 [8192, 512], P('rep'), may hold values from -1 to 1
- value_weight: bfloat16 [8192, 512], P('rep'), may hold values from -0.0625 to 0.0625
- w_out: bfloat16 [4096, 8192], P('rep', 'tp'), may hold values from -0.09375 to 0.09375
Outputs:
- mixed: bfloat16 [16384, 8192], P('rep', 'tp')
The draws below stay inside these ranges and needn't reach their ends.
All inputs are finite; a program needn't handle non-finite values.
Results may differ from the reference program's by a relative error of at most 0.011.
Values may be sent and summed in bfloat16 or wider, within the bound.
A program may use at most 128 MiB of HBM per device.

```python
import jax
import jax.numpy as jnp
from jax import lax

MODEL_WIDTH = 8192
QUERY_HEADS = 32
KEY_VALUE_HEADS = 4
HEAD_DIMENSION = 128
BLOCK_TOKENS = 512
TOKENS = 16384
N_REP = 32


def query_base(key):
    return jax.random.normal(key, (MODEL_WIDTH, QUERY_HEADS * HEAD_DIMENSION), jnp.float32)


def draw_w_query(key, part):
    base_offset = query_base(key)
    return (base_offset * MODEL_WIDTH ** (-0.5)).astype(jnp.bfloat16)


def draw_w_key(key, part):
    key = jax.random.fold_in(key, 2)
    value_rows = jax.random.normal(key, (MODEL_WIDTH, KEY_VALUE_HEADS * HEAD_DIMENSION), jnp.float32) * MODEL_WIDTH ** (-0.5)
    return value_rows.astype(jnp.bfloat16)


def shard_levels(own_key, extent, shards, smallest, largest):
    def one(dim, shards_of):
        draws = jax.random.uniform(jax.random.fold_in(jax.random.fold_in(own_key, 6), dim), (shards_of,), jnp.float32, smallest / len(shards), largest / len(shards))
        return jnp.repeat(jnp.exp(draws), extent[dim] // shards_of).reshape((-1,) + (1,) * (len(extent) - dim - 1))

    gain = one(*shards[0])
    for cut in shards[1:]:
        gain = gain * one(*cut)
    return gain


def centred(rng, extent, width, most, split=(), held_as=jnp.bfloat16):
    array = jax.random.normal(rng, extent, jnp.float32) * width
    if len(split) > 0:
        array = shard_levels(rng, extent, split, -0.22, 0.18) * array
    return jnp.clip(array, min=-most, max=most).astype(held_as)


def setup_inputs(seed: int = 0) -> dict:
    seeds = jax.random.split(jax.random.key(seed), 6)
    tokens = centred(seeds[0], (TOKENS, MODEL_WIDTH), 1.0, 6.0, ((0, 32),))
    w_query = draw_w_query(jax.random.fold_in(seeds[5], 71), 0)
    w_key = draw_w_key(jax.random.fold_in(seeds[5], 71), 0)
    value_weight = centred(seeds[3], (MODEL_WIDTH, KEY_VALUE_HEADS * HEAD_DIMENSION), MODEL_WIDTH ** -0.5, 0.0625, ((0, 32),))
    w_out = centred(seeds[4], (QUERY_HEADS * HEAD_DIMENSION, MODEL_WIDTH), (QUERY_HEADS * HEAD_DIMENSION) ** -0.5, 0.09375, ((0, 32), (1, 8)))
    return dict(tokens=tokens, w_query=w_query, w_key=w_key, value_weight=value_weight, w_out=w_out)


def apply_rotary(field, heads):
    rows = field.shape[0]
    shaped = field.reshape(rows, heads, HEAD_DIMENSION)
    positions = jnp.arange(rows, dtype=jnp.float32)
    freqs = 1000000.0 ** (-(jnp.arange(HEAD_DIMENSION // 2, dtype=jnp.float32) * 2.0 / HEAD_DIMENSION))
    angles = positions[:, None] * freqs[None, :]
    cosine = jnp.cos(angles)[:, None, :]
    sine = jnp.sin(angles)[:, None, :]
    first = shaped[:, :, :HEAD_DIMENSION // 2]
    second = shaped[:, :, HEAD_DIMENSION // 2:]
    turned = jnp.concatenate([first * cosine - second * sine, second * cosine + first * sine], axis=2)
    return turned.reshape(rows, heads * HEAD_DIMENSION)

def one_block(block, w_query, w_key, value_weight, w_out):
    widened = block.astype(jnp.float32)
    scale = lax.rsqrt(lax.optimization_barrier(jnp.mean(widened * widened, axis=1, keepdims=True)) + 1e-06)
    normed = (widened * scale).astype(jnp.bfloat16)
    query_state = jnp.dot(normed, w_query, preferred_element_type=jnp.float32)
    key_rows = jnp.dot(normed, w_key, preferred_element_type=jnp.float32)
    value_state = jnp.dot(normed, value_weight, preferred_element_type=jnp.float32).astype(jnp.bfloat16)
    query_state = apply_rotary(query_state, QUERY_HEADS).astype(jnp.bfloat16)
    key_rows = apply_rotary(key_rows, KEY_VALUE_HEADS).astype(jnp.bfloat16)
    group_index = QUERY_HEADS // KEY_VALUE_HEADS
    query_head_rows = query_state.astype(jnp.float32).reshape(BLOCK_TOKENS, KEY_VALUE_HEADS, group_index, HEAD_DIMENSION)
    key_head_rows = key_rows.astype(jnp.float32).reshape(BLOCK_TOKENS, KEY_VALUE_HEADS, HEAD_DIMENSION)
    value_head_rows = value_state.astype(jnp.float32).reshape(BLOCK_TOKENS, KEY_VALUE_HEADS, HEAD_DIMENSION)
    scores = jnp.einsum('qgjd,kgd->gjqk', query_head_rows, key_head_rows) / jnp.sqrt(jnp.float32(HEAD_DIMENSION))
    causal = jnp.arange(BLOCK_TOKENS)[:, None] >= jnp.arange(BLOCK_TOKENS)[None, :]
    scores = jnp.where(causal[None, None], scores, jnp.float32(-1e+30))
    top = lax.optimization_barrier(jnp.max(scores, axis=3, keepdims=True))
    expo = jnp.exp(scores - top)
    weights = (expo / lax.optimization_barrier(jnp.sum(expo, axis=3, keepdims=True))).astype(jnp.bfloat16)
    heads = jnp.einsum('gjqk,kgd->qgjd', weights.astype(jnp.float32), value_head_rows)
    heads = heads.reshape(BLOCK_TOKENS, QUERY_HEADS * HEAD_DIMENSION).astype(jnp.bfloat16)
    projected = jnp.dot(heads, w_out, preferred_element_type=jnp.float32)
    return (widened + projected).astype(jnp.bfloat16)

def reference(tokens, w_query, w_key, value_weight, w_out):
    blocks = tokens.reshape(N_REP, BLOCK_TOKENS, MODEL_WIDTH)
    mixed = lax.map(lambda block: one_block(block, w_query, w_key, value_weight, w_out), blocks)
    return mixed.reshape(N_REP * BLOCK_TOKENS, MODEL_WIDTH)
```

```python
import functools

import jax
import jax.numpy as jnp
import numpy as np
from jax import lax
from jax.experimental import pallas as pl
from jax.experimental.pallas import tpu as pltpu
from jax.sharding import PartitionSpec as P

MESH = pl.DeviceIdType.MESH
HEAD = 128
TOK = 512
WIDTH = 8192
FEATURES = 4096
HEADS = 4
OUT_COLS = 256
OUT_CHUNKS = 4
CHUNKS = 1 + HEADS + OUT_CHUNKS
SEMS = 160


def rotary_tables():
    pos = np.arange(TOK, dtype=np.float32)
    freqs = (1000000.0 ** (-(np.arange(HEAD // 2, dtype=np.float64) * 2.0 / HEAD))).astype(np.float32)
    angles = (pos[:, None] * freqs[None, :]).astype(np.float32).astype(np.float64)
    cosine, sine = np.cos(angles), np.sin(angles)
    return (
        np.concatenate([cosine, cosine], axis=1).astype(np.float32),
        np.concatenate([-sine, sine], axis=1).astype(np.float32),
    )


def kernel(tok_hbm, wq_hbm, wk_hbm, wv_hbm, wo_hbm, cos_hbm, sin_hbm, out_hbm,
           tok, wkv, wq, wo, heads, kv, res, cosv, sinv, outv, scale, ss, rs, ls):
    r = lax.axis_index("rep")
    t = lax.axis_index("tp")
    c, x, z = lax.rem(r, 2), lax.rem(lax.div(r, 2), 4), lax.div(r, 8)
    y, zh = lax.rem(t, 4), lax.div(t, 4)

    def at(z_, x_, c_):
        return ((z_ * 4 + x_) * 2 + c_, t)

    def at_tp(zh_, y_):
        return (r, zh_ * 4 + y_)

    def mod4(v):
        return lax.rem(v, 4)

    right, left, far = mod4(x + 1), mod4(x + 3), mod4(x + 2)
    sibling = at(z, x, 1 - c)
    to_right, to_left = at(z, right, c), at(z, left, c)
    z_peers = [at(mod4(z + d), x, c) for d in (1, 2, 3)]
    y_peers = [at_tp(zh, mod4(y + d)) for d in (1, 3, 2)]
    opposite = at_tp(1 - zh, y)
    parity = lax.rem(y, 2)
    y_pair = at_tp(zh, y + 1 - 2 * parity)

    def buf(k):
        if k == 0:
            return wkv
        if k <= HEADS:
            return wq.at[k - 1]
        return wo.at[k - 1 - HEADS]

    kv_col = pl.multiple_of(lax.div(t, 2) * HEAD, HEAD)
    own = []
    for k in range(CHUNKS):
        dst = buf(k).at[z, x, c]
        if k == 0:
            copy_k = pltpu.make_async_copy(wk_hbm.at[:, pl.ds(kv_col, HEAD)], dst, ls.at[0])
            copy_v = pltpu.make_async_copy(wv_hbm.at[:, pl.ds(kv_col, HEAD)], dst, ls.at[0])
            pl.when(parity == 0)(copy_k.start)
            pl.when(parity == 1)(copy_v.start)
            own.append(copy_k)
            continue
        if k <= HEADS:
            src = wq_hbm.at[:, pl.ds((k - 1) * HEAD, HEAD)]
        else:
            src = wo_hbm.at[:, pl.ds((k - 1 - HEADS) * OUT_COLS, OUT_COLS)]
        copy = pltpu.make_async_copy(src, dst, ls.at[k])
        copy.start()
        own.append(copy)
    load_tok = pltpu.make_async_copy(tok_hbm, tok, ls.at[CHUNKS])
    load_tok.start()
    res_col = pl.multiple_of(t * (OUT_COLS * OUT_CHUNKS), OUT_COLS)
    load_res = pltpu.make_async_copy(
        tok_hbm.at[:, pl.ds(res_col, OUT_COLS * OUT_CHUNKS)], res, ls.at[CHUNKS + 1]
    )
    load_cos = pltpu.make_async_copy(cos_hbm, cosv, ls.at[CHUNKS + 2])
    load_sin = pltpu.make_async_copy(sin_hbm, sinv, ls.at[CHUNKS + 3])
    for copy in (load_res, load_cos, load_sin):
        copy.start()

    barrier = pltpu.get_barrier_semaphore()
    partners = [sibling, to_right, to_left, *z_peers, *y_peers, opposite]
    for partner in partners:
        pl.semaphore_signal(barrier, inc=1, device_id=partner, device_id_type=MESH)
    pl.semaphore_wait(barrier, len(partners))

    sent = []

    def send(src, dst, device):
        i = len(sent)
        copy = pltpu.make_async_remote_copy(
            src_ref=src, dst_ref=dst, send_sem=ss.at[i], recv_sem=rs.at[i],
            device_id=device, device_id_type=MESH,
        )
        copy.start()
        sent.append(copy)
        return copy

    along_z, along_x, forwarded, across = {}, {}, {}, {}

    def z_send(k):
        own[k].wait()
        block = buf(k).at[z, x, c]
        along_z[k] = [send(block, block, peer) for peer in z_peers]

    def x_send(k):
        for copy in along_z[k]:
            copy.wait_recv()
        column = buf(k).at[:, x, c]
        along_x[k] = [send(column, column, to_right), send(column, column, to_left)]
        across[k] = [send(column, column, sibling)]

    def x_forward(k):
        from_left, from_right = buf(k).at[:, left, c], buf(k).at[:, right, c]
        along_x[k][0].wait_recv()
        low = buf(k).at[pl.ds(0, 2), left, c]
        forwarded[k] = [send(low, low, to_right)]
        across[k].append(send(from_left, from_left, sibling))
        along_x[k][1].wait_recv()
        high = buf(k).at[pl.ds(2, 2), right, c]
        forwarded[k].append(send(high, high, to_left))
        across[k].append(send(from_right, from_right, sibling))

    def finish(k):
        for copy in forwarded[k]:
            copy.wait_recv()
        last = buf(k).at[:, far, c]
        across[k].append(send(last, last, sibling))

    def arrived(k):
        for copy in across[k]:
            copy.wait_recv()

    def rotate(field):
        return field * cosv[...] + pltpu.roll(field, HEAD // 2, 1) * sinv[...]

    def statistics():
        load_tok.wait()

        @pl.loop(0, TOK // 32)
        def _(i):
            rows = pl.ds(pl.multiple_of(i * 32, 32), 32)
            wide = tok[rows, :].astype(jnp.float32)
            mean = jnp.sum(wide * wide, axis=1, keepdims=True) * (1.0 / WIDTH)
            scale[rows, :] = jnp.broadcast_to(lax.rsqrt(mean + 1e-6), (32, HEAD))

    def project(weights):
        product = jnp.dot(
            tok[...], weights[...].reshape(WIDTH, HEAD), preferred_element_type=jnp.float32
        )
        return product * scale[...]

    pair = []

    def key_or_value():
        for copy in (load_cos, load_sin):
            copy.wait()
        field = project(wkv)
        kv[parity] = jnp.where(parity == 0, rotate(field), field).astype(jnp.bfloat16)
        pair.append(send(kv.at[parity], kv.at[parity], y_pair))

    def head_block(zh_, y_, h):
        col = pl.multiple_of(((zh_ * 4 + y_) * HEADS + h) * HEAD, HEAD)
        return heads.at[:, pl.ds(col, HEAD)]

    near_heads, far_heads = {}, {}

    def attend(h):
        query = rotate(project(wq.at[h])).astype(jnp.bfloat16)
        if h == 0:
            pair[0].wait_recv()
        step = 128
        for i in range(TOK // step):
            extent = (i + 1) * step
            rows = query[i * step : extent, :]
            scores = lax.dot_general(
                rows, kv[0, :extent, :], (((1,), (1,)), ((), ())),
                preferred_element_type=jnp.float32,
            ) * (HEAD ** -0.5)
            q_pos = lax.broadcasted_iota(jnp.int32, (step, extent), 0) + i * step
            k_pos = lax.broadcasted_iota(jnp.int32, (step, extent), 1)
            scores = jnp.where(q_pos >= k_pos, scores, -1e30)
            expo = jnp.exp(scores - jnp.max(scores, axis=1, keepdims=True))
            weights = (expo / jnp.sum(expo, axis=1, keepdims=True)).astype(jnp.bfloat16)
            part = jnp.dot(weights, kv[1, :extent, :], preferred_element_type=jnp.float32)
            col = pl.multiple_of((t * HEADS + h) * HEAD, HEAD)
            heads[pl.ds(i * step, step), pl.ds(col, HEAD)] = part.astype(jnp.bfloat16)
        block = head_block(zh, y, h)
        near_heads[h] = [send(block, block, opposite)]
        near_heads[h] += [send(block, block, peer) for peer in y_peers]

    def pass_on(h):
        near_heads[h][0].wait_recv()
        block = head_block(1 - zh, y, h)
        far_heads[h] = [send(block, block, peer) for peer in y_peers]

    def gather_heads():
        for h in range(HEADS):
            for copy in near_heads[h][1:] + far_heads[h]:
                copy.wait_recv()

    stores = []

    def output(j):
        product = jnp.dot(
            heads[...], wo[j].reshape(FEATURES, OUT_COLS), preferred_element_type=jnp.float32
        )
        cols = pl.ds(j * OUT_COLS, OUT_COLS)
        outv[:, cols] = (res[:, cols].astype(jnp.float32) + product).astype(jnp.bfloat16)
        store = pltpu.make_async_copy(outv.at[:, cols], out_hbm.at[:, cols], ls.at[CHUNKS + 4 + j])
        store.start()
        stores.append(store)

    for k in range(3):
        z_send(k)
    x_send(0)
    statistics()
    x_send(1)
    for k in range(CHUNKS + 1):
        if k < CHUNKS:
            x_forward(k)
        if k + 3 < CHUNKS:
            z_send(k + 3)
        if k + 2 < CHUNKS:
            x_send(k + 2)
        if k >= 1:
            finish(k - 1)
            arrived(k - 1)
            if k - 1 == 0:
                key_or_value()
            elif k - 1 <= HEADS:
                h = k - 2
                attend(h)
                if h >= 1:
                    pass_on(h - 1)
            else:
                j = k - 2 - HEADS
                if j == 0:
                    pass_on(HEADS - 1)
                    load_res.wait()
                if j == 1:
                    gather_heads()
                    output(0)
                if j >= 1:
                    output(j)
    for copy in sent:
        copy.wait_send()
    for store in stores:
        store.wait()


def body(tokens, w_query, w_key, value_weight, w_out):
    cosine, sine = rotary_tables()
    any_space = pl.BlockSpec(memory_space=pl.ANY)
    blocks = (4, 4, 2)
    return pl.pallas_call(
        kernel,
        out_shape=jax.ShapeDtypeStruct((TOK, OUT_COLS * OUT_CHUNKS), jnp.bfloat16),
        in_specs=[any_space] * 7,
        out_specs=any_space,
        scratch_shapes=[
            pltpu.VMEM((TOK, WIDTH), jnp.bfloat16),
            pltpu.VMEM((*blocks, 256, HEAD), jnp.bfloat16),
            pltpu.VMEM((HEADS, *blocks, 256, HEAD), jnp.bfloat16),
            pltpu.VMEM((OUT_CHUNKS, *blocks, 128, OUT_COLS), jnp.bfloat16),
            pltpu.VMEM((TOK, FEATURES), jnp.bfloat16),
            pltpu.VMEM((2, TOK, HEAD), jnp.bfloat16),
            pltpu.VMEM((TOK, OUT_COLS * OUT_CHUNKS), jnp.bfloat16),
            pltpu.VMEM((TOK, HEAD), jnp.float32),
            pltpu.VMEM((TOK, HEAD), jnp.float32),
            pltpu.VMEM((TOK, OUT_COLS * OUT_CHUNKS), jnp.bfloat16),
            pltpu.VMEM((TOK, HEAD), jnp.float32),
            pltpu.SemaphoreType.DMA((SEMS,)),
            pltpu.SemaphoreType.DMA((SEMS,)),
            pltpu.SemaphoreType.DMA((CHUNKS + 4 + OUT_CHUNKS,)),
        ],
        compiler_params=pltpu.CompilerParams(
            collective_id=0, has_side_effects=True, vmem_limit_bytes=60 * 2**20
        ),
        cost_estimate=pl.CostEstimate(flops=11 * 10**9, bytes_accessed=12 * 2**20, transcendentals=2**20),
    )(tokens, w_query, w_key, value_weight, w_out, jnp.asarray(cosine), jnp.asarray(sine))


def solution(mesh):
    placed = (P("rep", None), P("rep", "tp"), P("rep", None), P("rep", None), P("rep", "tp"))
    return jax.shard_map(
        body, mesh=mesh, in_specs=placed, out_specs=P("rep", "tp"), check_vma=False
    )
```

```python
import functools

import jax
import jax.numpy as jnp
import numpy as np
from jax import lax
from jax.experimental import pallas as pl
from jax.experimental.pallas import tpu as pltpu
from jax.sharding import PartitionSpec as P

MESH = pl.DeviceIdType.MESH
HEAD = 128
TOK = 512
WIDTH = 8192
FEATURES = 4096
HEADS = 4
OUT_COLS = 256
OUT_CHUNKS = 4
PAIR = 2 * HEAD
PAIRS = HEADS // 2
CHUNKS = 1 + PAIRS + OUT_CHUNKS
ROWS = 128
SEMS = 160


def rotary_tables():
    pos = np.arange(TOK, dtype=np.float32)
    freqs = (1000000.0 ** (-(np.arange(HEAD // 2, dtype=np.float64) * 2.0 / HEAD))).astype(np.float32)
    angles = (pos[:, None] * freqs[None, :]).astype(np.float32).astype(np.float64)
    cosine, sine = np.cos(angles), np.sin(angles)
    return (
        np.concatenate([cosine, cosine], axis=1).astype(np.float32),
        np.concatenate([-sine, sine], axis=1).astype(np.float32),
    )


def kernel(tok_hbm, wq_hbm, wk_hbm, wv_hbm, wo_hbm, cos_hbm, sin_hbm, out_hbm,
           tok, wkv, wq, wo, heads, query, kv, res, cosv, sinv, outv, scale, ss, rs, ls):
    r = lax.axis_index("rep")
    t = lax.axis_index("tp")
    c, x, z = lax.rem(r, 2), lax.rem(lax.div(r, 2), 4), lax.div(r, 8)
    y, zh = lax.rem(t, 4), lax.div(t, 4)

    def at(z_, x_, c_):
        return ((z_ * 4 + x_) * 2 + c_, t)

    def at_tp(zh_, y_):
        return (r, zh_ * 4 + y_)

    def mod4(v):
        return lax.rem(v, 4)

    right, left, far = mod4(x + 1), mod4(x + 3), mod4(x + 2)
    sibling = at(z, x, 1 - c)
    to_right, to_left = at(z, right, c), at(z, left, c)
    z_peers = [at(mod4(z + d), x, c) for d in (1, 2, 3)]
    y_peers = [at_tp(zh, mod4(y + d)) for d in (1, 3)]
    opposite = at_tp(1 - zh, y)
    parity = lax.rem(y, 2)
    y_pair = at_tp(zh, y + 1 - 2 * parity)
    def buf(k):
        if k == 0:
            return wkv
        if k <= PAIRS:
            return wq.at[k - 1]
        return wo.at[k - 1 - PAIRS]

    kv_col = pl.multiple_of(lax.div(t, 2) * HEAD, HEAD)
    own = []
    for k in range(CHUNKS):
        dst = buf(k).at[0, x, c]
        if k == 0:
            copy_k = pltpu.make_async_copy(wk_hbm.at[:, pl.ds(kv_col, HEAD)], dst, ls.at[0])
            copy_v = pltpu.make_async_copy(wv_hbm.at[:, pl.ds(kv_col, HEAD)], dst, ls.at[0])
            pl.when(parity == 0)(copy_k.start)
            pl.when(parity == 1)(copy_v.start)
            own.append(copy_k)
            continue
        if k <= PAIRS:
            src = wq_hbm.at[:, pl.ds((k - 1) * PAIR, PAIR)]
        else:
            src = wo_hbm.at[:, pl.ds((k - 1 - PAIRS) * OUT_COLS, OUT_COLS)]
        copy = pltpu.make_async_copy(src, dst, ls.at[k])
        copy.start()
        own.append(copy)
    load_tok = []
    for slot in range(4):
        part = WIDTH // 4
        col = pl.multiple_of(mod4(z + slot) * part, part)
        copy = pltpu.make_async_copy(
            tok_hbm.at[:, pl.ds(col, part)], tok.at[:, pl.ds(slot * part, part)], ls.at[CHUNKS + slot]
        )
        copy.start()
        load_tok.append(copy)
    res_col = pl.multiple_of(t * (OUT_COLS * OUT_CHUNKS), OUT_COLS)
    load_res = pltpu.make_async_copy(
        tok_hbm.at[:, pl.ds(res_col, OUT_COLS * OUT_CHUNKS)], res, ls.at[CHUNKS + 4]
    )
    load_cos = pltpu.make_async_copy(cos_hbm, cosv, ls.at[CHUNKS + 5])
    load_sin = pltpu.make_async_copy(sin_hbm, sinv, ls.at[CHUNKS + 6])
    for copy in (load_res, load_cos, load_sin):
        copy.start()

    barrier = pltpu.get_barrier_semaphore()
    partners = [sibling, to_right, to_left, *z_peers, *y_peers, opposite]
    for partner in partners:
        pl.semaphore_signal(barrier, inc=1, device_id=partner, device_id_type=MESH)
    pl.semaphore_wait(barrier, len(partners))

    sent = []

    def send(src, dst, device):
        i = len(sent)
        copy = pltpu.make_async_remote_copy(
            src_ref=src, dst_ref=dst, send_sem=ss.at[i], recv_sem=rs.at[i],
            device_id=device, device_id_type=MESH,
        )
        copy.start()
        sent.append(copy)
        return copy

    along_z, own_x, rest_x, forwarded, across = {}, {}, {}, {}, {}

    def z_send(k):
        b = buf(k)
        mine = b.at[0, x, c]
        along_z[k] = [send(mine, b.at[4 - d, x, c], z_peers[d - 1]) for d in (1, 3, 2)]

    def own_send(k):
        mine = buf(k).at[0, x, c]
        own_x[k] = [send(mine, mine, to_right), send(mine, mine, to_left)]

    def rest_send(k):
        for copy in along_z[k]:
            copy.wait_recv()
        rest = buf(k).at[pl.ds(1, 3), x, c]
        rest_x[k] = [send(rest, rest, to_right), send(rest, rest, to_left)]
        column = buf(k).at[:, x, c]
        across[k] = [send(column, column, sibling)]

    def own_forward(k):
        own_x[k][0].wait_recv()
        block = buf(k).at[0, left, c]
        forwarded[k] = [send(block, block, to_right)]
        own_x[k][1].wait_recv()

    def rest_forward(k):
        rest_x[k][0].wait_recv()
        block = buf(k).at[1, left, c]
        forwarded[k].append(send(block, block, to_right))
        rest_x[k][1].wait_recv()
        block = buf(k).at[pl.ds(2, 2), right, c]
        forwarded[k].append(send(block, block, to_left))
        for side in (left, right):
            column = buf(k).at[:, side, c]
            across[k].append(send(column, column, sibling))

    def finish(k):
        for copy in forwarded[k]:
            copy.wait_recv()
        last = buf(k).at[:, far, c]
        across[k].append(send(last, last, sibling))
        for copy in across[k]:
            copy.wait_recv()

    def statistics():
        for copy in load_tok:
            copy.wait()

        @pl.loop(0, TOK // 32)
        def _(i):
            rows = pl.ds(pl.multiple_of(i * 32, 32), 32)
            wide = tok[rows, :].astype(jnp.float32)
            mean = jnp.sum(wide * wide, axis=1, keepdims=True) * (1.0 / WIDTH)
            scale[rows, :] = jnp.broadcast_to(lax.rsqrt(mean + 1e-6), (32, HEAD))

    def rotate(field, rows):
        return field * cosv[rows, :] + pltpu.roll(field, HEAD // 2, 1) * sinv[rows, :]

    def row_blocks(step):
        def run(work):
            @pl.loop(0, TOK // step)
            def _(i):
                work(pl.ds(pl.multiple_of(i * step, step), step))
        return run

    pair = []

    def key_or_value():
        for copy in (load_cos, load_sin):
            copy.wait()

        @row_blocks(ROWS)
        def _(rows):
            field = jnp.dot(
                tok[rows, :], wkv[...].reshape(WIDTH, HEAD), preferred_element_type=jnp.float32
            ) * scale[rows, :]
            kv[parity, rows, :] = jnp.where(parity == 0, rotate(field, rows), field).astype(jnp.bfloat16)

        pair.append(send(kv.at[parity], kv.at[parity], y_pair))

    def head_col(zh_, y_, h):
        owner = zh_ * 4 + y_
        slot = mod4(lax.div(owner, 2) - z + 4)
        return pl.multiple_of((slot * 8 + lax.rem(owner, 2) * HEADS + h) * HEAD, HEAD)

    near_heads, far_heads, last_heads = {}, {}, []

    def attend(p):
        @row_blocks(ROWS)
        def _(rows):
            product = jnp.dot(
                tok[rows, :], wq[p].reshape(WIDTH, PAIR), preferred_element_type=jnp.float32
            )
            for h in range(2):
                cols = slice(h * HEAD, (h + 1) * HEAD)
                field = product[:, cols] * scale[rows, :]
                query[rows, cols] = rotate(field, rows).astype(jnp.bfloat16)

        if p == 0:
            pair[0].wait_recv()
        step = 256
        blocks = [(h, i) for h in range(2) for i in range(TOK // step)]
        scores = []
        for h, i in blocks:
            extent = (i + 1) * step
            score = lax.dot_general(
                query[i * step : extent, h * HEAD : (h + 1) * HEAD], kv[0, :extent, :],
                (((1,), (1,)), ((), ())), preferred_element_type=jnp.float32,
            ) * (HEAD ** -0.5)
            q_pos = lax.broadcasted_iota(jnp.int32, (step, extent), 0) + i * step
            k_pos = lax.broadcasted_iota(jnp.int32, (step, extent), 1)
            scores.append(jnp.where(q_pos >= k_pos, score, -1e30))
        parts = []
        for (h, i), score in zip(blocks, scores):
            expo = jnp.exp(score - jnp.max(score, axis=1, keepdims=True))
            total = jnp.sum(expo, axis=1, keepdims=True)
            part = jnp.dot(
                expo.astype(jnp.bfloat16), kv[1, : (i + 1) * step, :],
                preferred_element_type=jnp.float32,
            )
            parts.append((part * (1.0 / total)).astype(jnp.bfloat16))
        for (h, i), part in zip(blocks, parts):
            heads[i * step : (i + 1) * step, pl.ds(head_col(zh, y, 2 * p + h), HEAD)] = part
        block = heads.at[:, pl.ds(head_col(zh, y, 2 * p), PAIR)]
        near_heads[p] = [send(block, block, opposite)]

    def share(p):
        block = heads.at[:, pl.ds(head_col(zh, y, 2 * p), PAIR)]
        near_heads[p] += [send(block, block, peer) for peer in y_peers]

    def relay_heads(p, near):
        pairs_of = (near_heads if near else far_heads)[p]
        first = 1 if near else 0
        side = zh if near else 1 - zh
        for i, (y_, device, half) in enumerate(((mod4(y + 3), y_peers[0], 0), (mod4(y + 1), y_peers[1], 1))):
            pairs_of[first + i].wait_recv()
            rows = pl.ds(half * (TOK // 2), TOK // 2)
            block = heads.at[rows, pl.ds(head_col(side, y_, 2 * p), PAIR)]
            last_heads.append(send(block, block, device))

    def pass_on(p):
        near_heads[p][0].wait_recv()
        block = heads.at[:, pl.ds(head_col(1 - zh, y, 2 * p), PAIR)]
        far_heads[p] = [send(block, block, peer) for peer in y_peers]

    def gather_heads():
        for copy in last_heads:
            copy.wait_recv()

    stores = []

    def output(j):
        cols = pl.ds(j * OUT_COLS, OUT_COLS)

        @row_blocks(ROWS)
        def _(rows):
            product = jnp.dot(
                heads[rows, :], wo[j].reshape(FEATURES, OUT_COLS), preferred_element_type=jnp.float32
            )
            outv[rows, cols] = (res[rows, cols].astype(jnp.float32) + product).astype(jnp.bfloat16)

        store = pltpu.make_async_copy(outv.at[:, cols], out_hbm.at[:, cols], ls.at[CHUNKS + 7 + j])
        store.start()
        stores.append(store)

    own[0].wait()
    z_send(0)
    own_send(0)
    own[1].wait()
    z_send(1)
    own_send(1)
    own[2].wait()
    z_send(2)
    own_send(2)
    for k in range(3, CHUNKS):
        own[k].wait()
        z_send(k)
    statistics()
    own_forward(0)
    rest_send(0)
    own_send(3)
    own_forward(1)
    own_forward(2)
    rest_forward(0)
    own_send(4)
    rest_send(1)
    own_forward(3)
    finish(0)
    key_or_value()
    own_forward(4)
    own_send(5)
    rest_forward(1)
    rest_send(2)
    finish(1)
    attend(0)
    share(0)
    own_send(6)
    own_forward(5)
    rest_forward(2)
    rest_send(3)
    relay_heads(0, True)
    own_forward(6)
    finish(2)
    rest_send(4)
    attend(1)
    share(1)
    rest_forward(3)
    pass_on(0)
    rest_send(5)
    finish(3)
    rest_forward(4)
    rest_send(6)
    relay_heads(0, False)
    relay_heads(1, True)
    finish(4)
    pass_on(1)
    rest_forward(5)
    load_res.wait()
    finish(5)
    relay_heads(1, False)
    rest_forward(6)
    gather_heads()
    output(0)
    output(1)
    output(2)
    finish(6)
    output(3)
    for copy in sent:
        copy.wait_send()
    for store in stores:
        store.wait()


def body(tokens, w_query, w_key, value_weight, w_out):
    cosine, sine = rotary_tables()
    any_space = pl.BlockSpec(memory_space=pl.ANY)
    blocks = (4, 4, 2)
    return pl.pallas_call(
        kernel,
        out_shape=jax.ShapeDtypeStruct((TOK, OUT_COLS * OUT_CHUNKS), jnp.bfloat16),
        in_specs=[any_space] * 7,
        out_specs=any_space,
        scratch_shapes=[
            pltpu.VMEM((TOK, WIDTH), jnp.bfloat16),
            pltpu.VMEM((*blocks, 256, HEAD), jnp.bfloat16),
            pltpu.VMEM((PAIRS, *blocks, 256, PAIR), jnp.bfloat16),
            pltpu.VMEM((OUT_CHUNKS, *blocks, 128, OUT_COLS), jnp.bfloat16),
            pltpu.VMEM((TOK, FEATURES), jnp.bfloat16),
            pltpu.VMEM((TOK, PAIR), jnp.bfloat16),
            pltpu.VMEM((2, TOK, HEAD), jnp.bfloat16),
            pltpu.VMEM((TOK, OUT_COLS * OUT_CHUNKS), jnp.bfloat16),
            pltpu.VMEM((TOK, HEAD), jnp.float32),
            pltpu.VMEM((TOK, HEAD), jnp.float32),
            pltpu.VMEM((TOK, OUT_COLS * OUT_CHUNKS), jnp.bfloat16),
            pltpu.VMEM((TOK, HEAD), jnp.float32),
            pltpu.SemaphoreType.DMA((SEMS,)),
            pltpu.SemaphoreType.DMA((SEMS,)),
            pltpu.SemaphoreType.DMA((CHUNKS + 7 + OUT_CHUNKS,)),
        ],
        compiler_params=pltpu.CompilerParams(
            collective_id=0, has_side_effects=True, vmem_limit_bytes=60 * 2**20
        ),
        cost_estimate=pl.CostEstimate(flops=11 * 10**9, bytes_accessed=12 * 2**20, transcendentals=2**20),
    )(tokens, w_query, w_key, value_weight, w_out, jnp.asarray(cosine), jnp.asarray(sine))


def solution(mesh):
    placed = (P("rep", None), P("rep", "tp"), P("rep", None), P("rep", None), P("rep", "tp"))
    return jax.shard_map(
        body, mesh=mesh, in_specs=placed, out_specs=P("rep", "tp"), check_vma=False
    )
```

```python
import functools

import jax
import jax.numpy as jnp
import numpy as np
from jax import lax
from jax.experimental import pallas as pl
from jax.experimental.pallas import tpu as pltpu
from jax.sharding import PartitionSpec as P

MESH = pl.DeviceIdType.MESH
HEAD = 128
TOK = 512
WIDTH = 8192
FEATURES = 4096
HEADS = 4
OUT_COLS = 256
OUT_CHUNKS = 4
PAIR = 2 * HEAD
PAIRS = HEADS // 2
CHUNKS = 1 + PAIRS + OUT_CHUNKS
ROWS = 128
SEMS = 160


def rotary_tables():
    pos = np.arange(TOK, dtype=np.float32)
    freqs = (1000000.0 ** (-(np.arange(HEAD // 2, dtype=np.float64) * 2.0 / HEAD))).astype(np.float32)
    angles = (pos[:, None] * freqs[None, :]).astype(np.float32).astype(np.float64)
    cosine, sine = np.cos(angles), np.sin(angles)
    return (
        np.concatenate([cosine, cosine], axis=1).astype(np.float32),
        np.concatenate([-sine, sine], axis=1).astype(np.float32),
    )


def kernel(tok_hbm, wq_hbm, wk_hbm, wv_hbm, wo_hbm, cos_hbm, sin_hbm, out_hbm,
           tok, wkv, wq, wo, heads, query, kv, res, cosv, sinv, outv, total, scale, ss, rs, ls):
    r = lax.axis_index("rep")
    t = lax.axis_index("tp")
    c, x, z = lax.rem(r, 2), lax.rem(lax.div(r, 2), 4), lax.div(r, 8)
    y, zh = lax.rem(t, 4), lax.div(t, 4)

    def at(z_, x_, c_):
        return ((z_ * 4 + x_) * 2 + c_, t)

    def at_tp(zh_, y_):
        return (r, zh_ * 4 + y_)

    def mod4(v):
        return lax.rem(v, 4)

    right, left, far = mod4(x + 1), mod4(x + 3), mod4(x + 2)
    sibling = at(z, x, 1 - c)
    to_right, to_left = at(z, right, c), at(z, left, c)
    z_peers = [at(mod4(z + d), x, c) for d in (1, 2, 3)]
    y_peers = [at_tp(zh, mod4(y + d)) for d in (1, 3)]
    opposite = at_tp(1 - zh, y)
    parity = lax.rem(y, 2)
    y_pair = at_tp(zh, y + 1 - 2 * parity)
    def buf(k):
        if k == 0:
            return wkv
        if k <= PAIRS:
            return wq.at[k - 1]
        return wo.at[k - 1 - PAIRS]

    kv_col = pl.multiple_of(lax.div(t, 2) * HEAD, HEAD)
    own = []
    for k in range(CHUNKS):
        dst = buf(k).at[0, x, c]
        if k == 0:
            copy_k = pltpu.make_async_copy(wk_hbm.at[:, pl.ds(kv_col, HEAD)], dst, ls.at[0])
            copy_v = pltpu.make_async_copy(wv_hbm.at[:, pl.ds(kv_col, HEAD)], dst, ls.at[0])
            pl.when(parity == 0)(copy_k.start)
            pl.when(parity == 1)(copy_v.start)
            own.append(copy_k)
            continue
        if k <= PAIRS:
            src = wq_hbm.at[:, pl.ds((k - 1) * PAIR, PAIR)]
        else:
            src = wo_hbm.at[:, pl.ds((k - 1 - PAIRS) * OUT_COLS, OUT_COLS)]
        copy = pltpu.make_async_copy(src, dst, ls.at[k])
        copy.start()
        own.append(copy)
    load_tok = []
    for slot in range(4):
        part = WIDTH // 4
        col = pl.multiple_of(mod4(z + slot) * part, part)
        copy = pltpu.make_async_copy(
            tok_hbm.at[:, pl.ds(col, part)], tok.at[:, pl.ds(slot * part, part)], ls.at[CHUNKS + slot]
        )
        copy.start()
        load_tok.append(copy)
    res_col = pl.multiple_of(t * (OUT_COLS * OUT_CHUNKS), OUT_COLS)
    load_res = pltpu.make_async_copy(
        tok_hbm.at[:, pl.ds(res_col, OUT_COLS * OUT_CHUNKS)], res, ls.at[CHUNKS + 4]
    )
    load_cos = pltpu.make_async_copy(cos_hbm, cosv, ls.at[CHUNKS + 5])
    load_sin = pltpu.make_async_copy(sin_hbm, sinv, ls.at[CHUNKS + 6])
    for copy in (load_res, load_cos, load_sin):
        copy.start()

    barrier = pltpu.get_barrier_semaphore()
    partners = [sibling, to_right, to_left, *z_peers, *y_peers, opposite]
    for partner in partners:
        pl.semaphore_signal(barrier, inc=1, device_id=partner, device_id_type=MESH)
    pl.semaphore_wait(barrier, len(partners))

    sent = []

    def send(src, dst, device):
        i = len(sent)
        copy = pltpu.make_async_remote_copy(
            src_ref=src, dst_ref=dst, send_sem=ss.at[i], recv_sem=rs.at[i],
            device_id=device, device_id_type=MESH,
        )
        copy.start()
        sent.append(copy)
        return copy

    along_z, own_x, rest_x, forwarded, across = {}, {}, {}, {}, {}

    def z_send(k):
        b = buf(k)
        mine = b.at[0, x, c]
        along_z[k] = [send(mine, b.at[4 - d, x, c], z_peers[d - 1]) for d in (1, 3, 2)]

    def own_send(k):
        mine = buf(k).at[0, x, c]
        own_x[k] = [send(mine, mine, to_right), send(mine, mine, to_left)]

    def rest_send(k):
        for copy in along_z[k]:
            copy.wait_recv()
        rest = buf(k).at[pl.ds(1, 3), x, c]
        rest_x[k] = [send(rest, rest, to_right), send(rest, rest, to_left)]
        column = buf(k).at[:, x, c]
        across[k] = [send(column, column, sibling)]

    def own_forward(k):
        own_x[k][0].wait_recv()
        block = buf(k).at[0, left, c]
        forwarded[k] = [send(block, block, to_right)]
        own_x[k][1].wait_recv()

    def rest_forward(k):
        rest_x[k][0].wait_recv()
        block = buf(k).at[1, left, c]
        forwarded[k].append(send(block, block, to_right))
        rest_x[k][1].wait_recv()
        block = buf(k).at[pl.ds(2, 2), right, c]
        forwarded[k].append(send(block, block, to_left))
        for side in (left, right):
            column = buf(k).at[:, side, c]
            across[k].append(send(column, column, sibling))

    def finish(k):
        for copy in forwarded[k]:
            copy.wait_recv()
        last = buf(k).at[:, far, c]
        across[k].append(send(last, last, sibling))
        for copy in across[k]:
            copy.wait_recv()

    def statistics():
        for copy in load_tok:
            copy.wait()

        @pl.loop(0, TOK // 32)
        def _(i):
            rows = pl.ds(pl.multiple_of(i * 32, 32), 32)
            wide = tok[rows, :].astype(jnp.float32)
            mean = jnp.sum(wide * wide, axis=1, keepdims=True) * (1.0 / WIDTH)
            scale[rows, :] = jnp.broadcast_to(lax.rsqrt(mean + 1e-6), (32, HEAD))

    def rotate(field, rows):
        return field * cosv[rows, :] + pltpu.roll(field, HEAD // 2, 1) * sinv[rows, :]

    def row_blocks(step):
        def run(work):
            @pl.loop(0, TOK // step)
            def _(i):
                work(pl.ds(pl.multiple_of(i * step, step), step))
        return run

    pair = []

    def key_or_value():
        for copy in (load_cos, load_sin):
            copy.wait()

        @row_blocks(ROWS)
        def _(rows):
            field = jnp.dot(
                tok[rows, :], wkv[...].reshape(WIDTH, HEAD), preferred_element_type=jnp.float32
            ) * scale[rows, :]
            kv[parity, rows, :] = jnp.where(parity == 0, rotate(field, rows), field).astype(jnp.bfloat16)

        pair.append(send(kv.at[parity], kv.at[parity], y_pair))

    def head_index(zh_, y_, p):
        owner = zh_ * 4 + y_
        slot = mod4(lax.div(owner, 2) - z + 4)
        return slot * 4 + lax.rem(owner, 2) * PAIRS + p

    near_heads, far_heads, last_heads = {}, {}, {}

    def attend(p):
        @row_blocks(ROWS)
        def _(rows):
            product = jnp.dot(
                tok[rows, :], wq[p].reshape(WIDTH, PAIR), preferred_element_type=jnp.float32
            )
            for h in range(2):
                cols = slice(h * HEAD, (h + 1) * HEAD)
                field = product[:, cols] * scale[rows, :]
                query[rows, cols] = rotate(field, rows).astype(jnp.bfloat16)

        if p == 0:
            pair[0].wait_recv()
        step = 256
        blocks = [(h, i) for h in range(2) for i in range(TOK // step)]
        scores = []
        for h, i in blocks:
            extent = (i + 1) * step
            score = lax.dot_general(
                query[i * step : extent, h * HEAD : (h + 1) * HEAD], kv[0, :extent, :],
                (((1,), (1,)), ((), ())), preferred_element_type=jnp.float32,
            ) * (HEAD ** -0.5)
            q_pos = lax.broadcasted_iota(jnp.int32, (step, extent), 0) + i * step
            k_pos = lax.broadcasted_iota(jnp.int32, (step, extent), 1)
            scores.append(jnp.where(q_pos >= k_pos, score, -1e30))
        parts = []
        for (h, i), score in zip(blocks, scores):
            expo = jnp.exp(score - jnp.max(score, axis=1, keepdims=True))
            norm = jnp.sum(expo, axis=1, keepdims=True)
            part = jnp.dot(
                expo.astype(jnp.bfloat16), kv[1, : (i + 1) * step, :],
                preferred_element_type=jnp.float32,
            )
            parts.append((part * (1.0 / norm)).astype(jnp.bfloat16))
        for (h, i), part in zip(blocks, parts):
            heads[head_index(zh, y, p), i * step : (i + 1) * step, h * HEAD : (h + 1) * HEAD] = part
        block = heads.at[head_index(zh, y, p)]
        near_heads[p] = [send(block, block, opposite)]

    def share(p):
        block = heads.at[head_index(zh, y, p)]
        near_heads[p] += [send(block, block, peer) for peer in y_peers]

    def relay_heads(p, near):
        pairs_of = (near_heads if near else far_heads)[p]
        first = 1 if near else 0
        side = zh if near else 1 - zh
        for i, (y_, device, half) in enumerate(((mod4(y + 3), y_peers[0], 0), (mod4(y + 1), y_peers[1], 1))):
            pairs_of[first + i].wait_recv()
            rows = pl.ds(half * (TOK // 2), TOK // 2)
            block = heads.at[head_index(side, y_, p), rows]
            last_heads.setdefault((p, near), []).append(send(block, block, device))

    def pass_on(p):
        near_heads[p][0].wait_recv()
        block = heads.at[head_index(1 - zh, y, p)]
        far_heads[p] = [send(block, block, peer) for peer in y_peers]

    def gather_heads(*keys):
        for key in keys:
            for copy in last_heads[key]:
                copy.wait_recv()

    stores = []

    def times(j, rows, indices):
        product = None
        for i in indices:
            block = wo[j, lax.div(i, 4), lax.rem(i, 4)].reshape(PAIR, OUT_COLS)
            term = jnp.dot(heads[i, rows, :], block, preferred_element_type=jnp.float32)
            product = term if product is None else product + term
        return product

    def output_most(j):
        cols = pl.ds(j * OUT_COLS, OUT_COLS)

        @row_blocks(ROWS)
        def _(rows):
            indices = [head_index(zh_, y_, 0) for zh_ in range(2) for y_ in range(4)]
            indices += [head_index(zh, y_, 1) for y_ in range(4)]
            total[rows, cols] = res[rows, cols].astype(jnp.float32) + times(j, rows, indices)

    def output(j):
        cols = pl.ds(j * OUT_COLS, OUT_COLS)

        @row_blocks(ROWS)
        def _(rows):
            indices = [head_index(1 - zh, y_, 1) for y_ in range(4)]
            outv[rows, cols] = (total[rows, cols] + times(j, rows, indices)).astype(jnp.bfloat16)

        store = pltpu.make_async_copy(outv.at[:, cols], out_hbm.at[:, cols], ls.at[CHUNKS + 7 + j])
        store.start()
        stores.append(store)

    own[0].wait()
    z_send(0)
    own_send(0)
    for k in range(1, CHUNKS):
        own[k].wait()
    own_send(1)
    own_send(2)
    rest_send(0)
    z_send(1)
    own_forward(0)
    own_send(3)
    own_forward(1)
    statistics()
    own_forward(2)
    rest_forward(0)
    own_send(4)
    rest_send(1)
    z_send(2)
    z_send(3)
    own_forward(3)
    finish(0)
    key_or_value()
    own_forward(4)
    own_send(5)
    rest_forward(1)
    rest_send(2)
    z_send(4)
    z_send(5)
    z_send(6)
    finish(1)
    attend(0)
    share(0)
    own_send(6)
    own_forward(5)
    rest_forward(2)
    rest_send(3)
    relay_heads(0, True)
    own_forward(6)
    finish(2)
    rest_send(4)
    attend(1)
    share(1)
    rest_forward(3)
    pass_on(0)
    rest_send(5)
    finish(3)
    rest_forward(4)
    rest_send(6)
    relay_heads(0, False)
    relay_heads(1, True)
    finish(4)
    pass_on(1)
    rest_forward(5)
    load_res.wait()
    finish(5)
    gather_heads((0, True), (0, False), (1, True))
    output_most(0)
    relay_heads(1, False)
    output_most(1)
    rest_forward(6)
    output_most(2)
    gather_heads((1, False))
    output(0)
    output(1)
    output(2)
    finish(6)
    output_most(3)
    output(3)
    for copy in sent:
        copy.wait_send()
    for store in stores:
        store.wait()


def body(tokens, w_query, w_key, value_weight, w_out):
    cosine, sine = rotary_tables()
    any_space = pl.BlockSpec(memory_space=pl.ANY)
    blocks = (4, 4, 2)
    return pl.pallas_call(
        kernel,
        out_shape=jax.ShapeDtypeStruct((TOK, OUT_COLS * OUT_CHUNKS), jnp.bfloat16),
        in_specs=[any_space] * 7,
        out_specs=any_space,
        scratch_shapes=[
            pltpu.VMEM((TOK, WIDTH), jnp.bfloat16),
            pltpu.VMEM((*blocks, 256, HEAD), jnp.bfloat16),
            pltpu.VMEM((PAIRS, *blocks, 256, PAIR), jnp.bfloat16),
            pltpu.VMEM((OUT_CHUNKS, *blocks, 128, OUT_COLS), jnp.bfloat16),
            pltpu.VMEM((FEATURES // PAIR, TOK, PAIR), jnp.bfloat16),
            pltpu.VMEM((TOK, PAIR), jnp.bfloat16),
            pltpu.VMEM((2, TOK, HEAD), jnp.bfloat16),
            pltpu.VMEM((TOK, OUT_COLS * OUT_CHUNKS), jnp.bfloat16),
            pltpu.VMEM((TOK, HEAD), jnp.float32),
            pltpu.VMEM((TOK, HEAD), jnp.float32),
            pltpu.VMEM((TOK, OUT_COLS * OUT_CHUNKS), jnp.bfloat16),
            pltpu.VMEM((TOK, OUT_COLS * OUT_CHUNKS), jnp.float32),
            pltpu.VMEM((TOK, HEAD), jnp.float32),
            pltpu.SemaphoreType.DMA((SEMS,)),
            pltpu.SemaphoreType.DMA((SEMS,)),
            pltpu.SemaphoreType.DMA((CHUNKS + 7 + OUT_CHUNKS,)),
        ],
        compiler_params=pltpu.CompilerParams(
            collective_id=0, has_side_effects=True, vmem_limit_bytes=60 * 2**20
        ),
        cost_estimate=pl.CostEstimate(flops=11 * 10**9, bytes_accessed=12 * 2**20, transcendentals=2**20),
    )(tokens, w_query, w_key, value_weight, w_out, jnp.asarray(cosine), jnp.asarray(sine))


def solution(mesh):
    placed = (P("rep", None), P("rep", "tp"), P("rep", None), P("rep", None), P("rep", "tp"))
    return jax.shard_map(
        body, mesh=mesh, in_specs=placed, out_specs=P("rep", "tp"), check_vma=False
    )
```

```python
import functools

import jax
import jax.numpy as jnp
import numpy as np
from jax import lax
from jax.experimental import pallas as pl
from jax.experimental.pallas import tpu as pltpu
from jax.sharding import PartitionSpec as P

MESH = pl.DeviceIdType.MESH
HEAD = 128
TOK = 512
WIDTH = 8192
FEATURES = 4096
HEADS = 4
OUT_COLS = 256
OUT_CHUNKS = 4
PAIR = 2 * HEAD
PAIRS = HEADS // 2
CHUNKS = 1 + PAIRS + OUT_CHUNKS
ROWS = 256
SEMS = 160


def rotary_tables():
    pos = np.arange(TOK, dtype=np.float32)
    freqs = (1000000.0 ** (-(np.arange(HEAD // 2, dtype=np.float64) * 2.0 / HEAD))).astype(np.float32)
    angles = (pos[:, None] * freqs[None, :]).astype(np.float32).astype(np.float64)
    cosine, sine = np.cos(angles), np.sin(angles)
    return (
        np.concatenate([cosine, cosine], axis=1).astype(np.float32),
        np.concatenate([-sine, sine], axis=1).astype(np.float32),
    )


def kernel(tok_hbm, wq_hbm, wk_hbm, wv_hbm, wo_hbm, cos_hbm, sin_hbm, out_hbm,
           tok, wkv, wq, wo, heads, query, kv, res, cosv, sinv, outv, total, scale, ss, rs, ls):
    r = lax.axis_index("rep")
    t = lax.axis_index("tp")
    c, x, z = lax.rem(r, 2), lax.rem(lax.div(r, 2), 4), lax.div(r, 8)
    y, zh = lax.rem(t, 4), lax.div(t, 4)

    def at(z_, x_, c_):
        return ((z_ * 4 + x_) * 2 + c_, t)

    def at_tp(zh_, y_):
        return (r, zh_ * 4 + y_)

    def mod4(v):
        return lax.rem(v, 4)

    right, left, far = mod4(x + 1), mod4(x + 3), mod4(x + 2)
    sibling = at(z, x, 1 - c)
    to_right, to_left = at(z, right, c), at(z, left, c)
    z_peers = [at(mod4(z + d), x, c) for d in (1, 2, 3)]
    y_peers = [at_tp(zh, mod4(y + d)) for d in (1, 3)]
    opposite = at_tp(1 - zh, y)
    parity = lax.rem(y, 2)
    y_pair = at_tp(zh, y + 1 - 2 * parity)
    def buf(k):
        if k == 0:
            return wkv
        if k <= PAIRS:
            return wq.at[k - 1]
        return wo.at[k - 1 - PAIRS]

    kv_col = pl.multiple_of(lax.div(t, 2) * HEAD, HEAD)
    own = []
    for k in range(CHUNKS):
        dst = buf(k).at[0, x, c]
        if k == 0:
            copy_k = pltpu.make_async_copy(wk_hbm.at[:, pl.ds(kv_col, HEAD)], dst, ls.at[0])
            copy_v = pltpu.make_async_copy(wv_hbm.at[:, pl.ds(kv_col, HEAD)], dst, ls.at[0])
            pl.when(parity == 0)(copy_k.start)
            pl.when(parity == 1)(copy_v.start)
            own.append(copy_k)
            continue
        if k <= PAIRS:
            src = wq_hbm.at[:, pl.ds((k - 1) * PAIR, PAIR)]
        else:
            src = wo_hbm.at[:, pl.ds((k - 1 - PAIRS) * OUT_COLS, OUT_COLS)]
        copy = pltpu.make_async_copy(src, dst, ls.at[k])
        copy.start()
        own.append(copy)
    load_tok = []
    for slot in range(4):
        part = WIDTH // 4
        col = pl.multiple_of(mod4(z + slot) * part, part)
        copy = pltpu.make_async_copy(
            tok_hbm.at[:, pl.ds(col, part)], tok.at[:, pl.ds(slot * part, part)], ls.at[CHUNKS + slot]
        )
        copy.start()
        load_tok.append(copy)
    res_col = pl.multiple_of(t * (OUT_COLS * OUT_CHUNKS), OUT_COLS)
    load_res = pltpu.make_async_copy(
        tok_hbm.at[:, pl.ds(res_col, OUT_COLS * OUT_CHUNKS)], res, ls.at[CHUNKS + 4]
    )
    load_cos = pltpu.make_async_copy(cos_hbm, cosv, ls.at[CHUNKS + 5])
    load_sin = pltpu.make_async_copy(sin_hbm, sinv, ls.at[CHUNKS + 6])
    for copy in (load_res, load_cos, load_sin):
        copy.start()

    barrier = pltpu.get_barrier_semaphore()
    partners = [sibling, to_right, to_left, *z_peers, *y_peers, opposite]
    for partner in partners:
        pl.semaphore_signal(barrier, inc=1, device_id=partner, device_id_type=MESH)
    pl.semaphore_wait(barrier, len(partners))

    sent = []

    def send(src, dst, device):
        i = len(sent)
        copy = pltpu.make_async_remote_copy(
            src_ref=src, dst_ref=dst, send_sem=ss.at[i], recv_sem=rs.at[i],
            device_id=device, device_id_type=MESH,
        )
        copy.start()
        sent.append(copy)
        return copy

    along_z, own_x, rest_x, forwarded, across = {}, {}, {}, {}, {}

    def z_send(k):
        b = buf(k)
        mine = b.at[0, x, c]
        along_z[k] = [send(mine, b.at[4 - d, x, c], z_peers[d - 1]) for d in (1, 3, 2)]

    def own_send(k):
        mine = buf(k).at[0, x, c]
        own_x[k] = [send(mine, mine, to_right), send(mine, mine, to_left)]

    def rest_send(k):
        for copy in along_z[k]:
            copy.wait_recv()
        rest = buf(k).at[pl.ds(1, 3), x, c]
        rest_x[k] = [send(rest, rest, to_right), send(rest, rest, to_left)]
        column = buf(k).at[:, x, c]
        across[k] = [send(column, column, sibling)]

    def own_forward(k):
        own_x[k][0].wait_recv()
        block = buf(k).at[0, left, c]
        forwarded[k] = [send(block, block, to_right)]
        own_x[k][1].wait_recv()

    def rest_forward(k):
        rest_x[k][0].wait_recv()
        block = buf(k).at[1, left, c]
        forwarded[k].append(send(block, block, to_right))
        rest_x[k][1].wait_recv()
        block = buf(k).at[pl.ds(2, 2), right, c]
        forwarded[k].append(send(block, block, to_left))
        for side in (left, right):
            column = buf(k).at[:, side, c]
            across[k].append(send(column, column, sibling))

    def finish(k):
        for copy in forwarded[k]:
            copy.wait_recv()
        last = buf(k).at[:, far, c]
        across[k].append(send(last, last, sibling))
        for copy in across[k]:
            copy.wait_recv()

    def statistics():
        for copy in load_tok:
            copy.wait()

        @pl.loop(0, TOK // 32)
        def _(i):
            rows = pl.ds(pl.multiple_of(i * 32, 32), 32)
            wide = tok[rows, :].astype(jnp.float32)
            mean = jnp.sum(wide * wide, axis=1, keepdims=True) * (1.0 / WIDTH)
            scale[rows, :] = jnp.broadcast_to(lax.rsqrt(mean + 1e-6), (32, HEAD))

    def rotate(field, rows):
        return field * cosv[rows, :] + pltpu.roll(field, HEAD // 2, 1) * sinv[rows, :]

    def row_blocks(step):
        def run(work):
            @pl.loop(0, TOK // step)
            def _(i):
                work(pl.ds(pl.multiple_of(i * step, step), step))
        return run

    pair = []

    def key_or_value():
        for copy in (load_cos, load_sin):
            copy.wait()

        @row_blocks(ROWS)
        def _(rows):
            field = jnp.dot(
                tok[rows, :], wkv[...].reshape(WIDTH, HEAD), preferred_element_type=jnp.float32
            ) * scale[rows, :]
            kv[parity, rows, :] = jnp.where(parity == 0, rotate(field, rows), field).astype(jnp.bfloat16)

        pair.append(send(kv.at[parity], kv.at[parity], y_pair))

    def head_index(zh_, y_, p):
        owner = zh_ * 4 + y_
        slot = mod4(lax.div(owner, 2) - z + 4)
        return slot * 4 + lax.rem(owner, 2) * PAIRS + p

    near_heads, far_heads, last_heads = {}, {}, {}

    def attend(p):
        @row_blocks(ROWS)
        def _(rows):
            product = jnp.dot(
                tok[rows, :], wq[p].reshape(WIDTH, PAIR), preferred_element_type=jnp.float32
            )
            for h in range(2):
                cols = slice(h * HEAD, (h + 1) * HEAD)
                field = product[:, cols] * scale[rows, :]
                query[rows, cols] = rotate(field, rows).astype(jnp.bfloat16)

        if p == 0:
            pair[0].wait_recv()
        step = 256
        blocks = [(h, i) for h in range(2) for i in range(TOK // step)]
        scores = []
        for h, i in blocks:
            extent = (i + 1) * step
            score = lax.dot_general(
                query[i * step : extent, h * HEAD : (h + 1) * HEAD], kv[0, :extent, :],
                (((1,), (1,)), ((), ())), preferred_element_type=jnp.float32,
            ) * (HEAD ** -0.5)
            q_pos = lax.broadcasted_iota(jnp.int32, (step, extent), 0) + i * step
            k_pos = lax.broadcasted_iota(jnp.int32, (step, extent), 1)
            scores.append(jnp.where(q_pos >= k_pos, score, -1e30))
        parts = []
        for (h, i), score in zip(blocks, scores):
            expo = jnp.exp(score - jnp.max(score, axis=1, keepdims=True))
            norm = jnp.sum(expo, axis=1, keepdims=True)
            part = jnp.dot(
                expo.astype(jnp.bfloat16), kv[1, : (i + 1) * step, :],
                preferred_element_type=jnp.float32,
            )
            parts.append((part * (1.0 / norm)).astype(jnp.bfloat16))
        for (h, i), part in zip(blocks, parts):
            heads[head_index(zh, y, p), i * step : (i + 1) * step, h * HEAD : (h + 1) * HEAD] = part
        block = heads.at[head_index(zh, y, p)]
        near_heads[p] = [send(block, block, opposite)]

    def share(p):
        block = heads.at[head_index(zh, y, p)]
        near_heads[p] += [send(block, block, peer) for peer in y_peers]

    def relay_heads(p, near):
        pairs_of = (near_heads if near else far_heads)[p]
        first = 1 if near else 0
        side = zh if near else 1 - zh
        for i, (y_, device, half) in enumerate(((mod4(y + 3), y_peers[0], 0), (mod4(y + 1), y_peers[1], 1))):
            pairs_of[first + i].wait_recv()
            rows = pl.ds(half * (TOK // 2), TOK // 2)
            block = heads.at[head_index(side, y_, p), rows]
            last_heads.setdefault((p, near), []).append(send(block, block, device))

    def pass_on(p):
        near_heads[p][0].wait_recv()
        block = heads.at[head_index(1 - zh, y, p)]
        far_heads[p] = [send(block, block, peer) for peer in y_peers]

    def gather_heads(*keys):
        for key in keys:
            for copy in last_heads[key]:
                copy.wait_recv()

    stores = []

    def times(j, rows, indices):
        product = None
        for i in indices:
            block = wo[j, lax.div(i, 4), lax.rem(i, 4)].reshape(PAIR, OUT_COLS)
            term = jnp.dot(heads[i, rows, :], block, preferred_element_type=jnp.float32)
            product = term if product is None else product + term
        return product

    def output_most(j):
        cols = pl.ds(j * OUT_COLS, OUT_COLS)

        @row_blocks(ROWS)
        def _(rows):
            indices = [head_index(zh_, y_, 0) for zh_ in range(2) for y_ in range(4)]
            indices += [head_index(zh, y_, 1) for y_ in range(4)]
            total[rows, cols] = res[rows, cols].astype(jnp.float32) + times(j, rows, indices)

    def output(j):
        cols = pl.ds(j * OUT_COLS, OUT_COLS)

        @row_blocks(ROWS)
        def _(rows):
            indices = [head_index(1 - zh, y_, 1) for y_ in range(4)]
            outv[rows, cols] = (total[rows, cols] + times(j, rows, indices)).astype(jnp.bfloat16)

        store = pltpu.make_async_copy(outv.at[:, cols], out_hbm.at[:, cols], ls.at[CHUNKS + 7 + j])
        store.start()
        stores.append(store)

    own[0].wait()
    z_send(0)
    own_send(0)
    for k in range(1, CHUNKS):
        own[k].wait()
    own_send(1)
    own_send(2)
    rest_send(0)
    z_send(1)
    own_forward(0)
    own_send(3)
    own_forward(1)
    statistics()
    own_forward(2)
    rest_forward(0)
    own_send(4)
    rest_send(1)
    z_send(2)
    z_send(3)
    own_forward(3)
    finish(0)
    key_or_value()
    own_forward(4)
    own_send(5)
    rest_forward(1)
    rest_send(2)
    z_send(4)
    z_send(5)
    z_send(6)
    finish(1)
    attend(0)
    share(0)
    own_send(6)
    own_forward(5)
    rest_forward(2)
    rest_send(3)
    relay_heads(0, True)
    own_forward(6)
    finish(2)
    rest_send(4)
    attend(1)
    share(1)
    rest_forward(3)
    pass_on(0)
    rest_send(5)
    finish(3)
    rest_forward(4)
    rest_send(6)
    relay_heads(0, False)
    relay_heads(1, True)
    finish(4)
    pass_on(1)
    rest_forward(5)
    load_res.wait()
    finish(5)
    gather_heads((0, True), (0, False), (1, True))
    output_most(0)
    relay_heads(1, False)
    output_most(1)
    rest_forward(6)
    output_most(2)
    gather_heads((1, False))
    output(0)
    output(1)
    output(2)
    finish(6)
    output_most(3)
    output(3)
    for copy in sent:
        copy.wait_send()
    for store in stores:
        store.wait()


def body(tokens, w_query, w_key, value_weight, w_out):
    cosine, sine = rotary_tables()
    any_space = pl.BlockSpec(memory_space=pl.ANY)
    blocks = (4, 4, 2)
    return pl.pallas_call(
        kernel,
        out_shape=jax.ShapeDtypeStruct((TOK, OUT_COLS * OUT_CHUNKS), jnp.bfloat16),
        in_specs=[any_space] * 7,
        out_specs=any_space,
        scratch_shapes=[
            pltpu.VMEM((TOK, WIDTH), jnp.bfloat16),
            pltpu.VMEM((*blocks, 256, HEAD), jnp.bfloat16),
            pltpu.VMEM((PAIRS, *blocks, 256, PAIR), jnp.bfloat16),
            pltpu.VMEM((OUT_CHUNKS, *blocks, 128, OUT_COLS), jnp.bfloat16),
            pltpu.VMEM((FEATURES // PAIR, TOK, PAIR), jnp.bfloat16),
            pltpu.VMEM((TOK, PAIR), jnp.bfloat16),
            pltpu.VMEM((2, TOK, HEAD), jnp.bfloat16),
            pltpu.VMEM((TOK, OUT_COLS * OUT_CHUNKS), jnp.bfloat16),
            pltpu.VMEM((TOK, HEAD), jnp.float32),
            pltpu.VMEM((TOK, HEAD), jnp.float32),
            pltpu.VMEM((TOK, OUT_COLS * OUT_CHUNKS), jnp.bfloat16),
            pltpu.VMEM((TOK, OUT_COLS * OUT_CHUNKS), jnp.float32),
            pltpu.VMEM((TOK, HEAD), jnp.float32),
            pltpu.SemaphoreType.DMA((SEMS,)),
            pltpu.SemaphoreType.DMA((SEMS,)),
            pltpu.SemaphoreType.DMA((CHUNKS + 7 + OUT_CHUNKS,)),
        ],
        compiler_params=pltpu.CompilerParams(
            collective_id=0, has_side_effects=True, vmem_limit_bytes=60 * 2**20
        ),
        cost_estimate=pl.CostEstimate(flops=11 * 10**9, bytes_accessed=12 * 2**20, transcendentals=2**20),
    )(tokens, w_query, w_key, value_weight, w_out, jnp.asarray(cosine), jnp.asarray(sine))


def solution(mesh):
    placed = (P("rep", None), P("rep", "tp"), P("rep", None), P("rep", None), P("rep", "tp"))
    return jax.shard_map(
        body, mesh=mesh, in_specs=placed, out_specs=P("rep", "tp"), check_vma=False
    )
```

```python
import functools

import jax
import jax.numpy as jnp
import numpy as np
from jax import lax
from jax.experimental import pallas as pl
from jax.experimental.pallas import tpu as pltpu
from jax.sharding import PartitionSpec as P

MESH = pl.DeviceIdType.MESH
HEAD = 128
TOK = 512
WIDTH = 8192
FEATURES = 4096
HEADS = 4
OUT_COLS = 256
OUT_CHUNKS = 4
PAIR = 2 * HEAD
PAIRS = HEADS // 2
CHUNKS = 1 + PAIRS + OUT_CHUNKS
ROWS = 256
SEMS = 160


def rotary_tables():
    pos = np.arange(TOK, dtype=np.float32)
    freqs = (1000000.0 ** (-(np.arange(HEAD // 2, dtype=np.float64) * 2.0 / HEAD))).astype(np.float32)
    angles = (pos[:, None] * freqs[None, :]).astype(np.float32).astype(np.float64)
    cosine, sine = np.cos(angles), np.sin(angles)
    return (
        np.concatenate([cosine, cosine], axis=1).astype(np.float32),
        np.concatenate([-sine, sine], axis=1).astype(np.float32),
    )


def kernel(tok_hbm, wq_hbm, wk_hbm, wv_hbm, wo_hbm, cos_hbm, sin_hbm, out_hbm,
           tok, wkv, wq, wo, heads, query, kv, res, cosv, sinv, outv, total, scale, ss, rs, ls):
    r = lax.axis_index("rep")
    t = lax.axis_index("tp")
    c, x, z = lax.rem(r, 2), lax.rem(lax.div(r, 2), 4), lax.div(r, 8)
    y, zh = lax.rem(t, 4), lax.div(t, 4)

    def at(z_, x_, c_):
        return ((z_ * 4 + x_) * 2 + c_, t)

    def at_tp(zh_, y_):
        return (r, zh_ * 4 + y_)

    def mod4(v):
        return lax.rem(v, 4)

    right, left, far = mod4(x + 1), mod4(x + 3), mod4(x + 2)
    sibling = at(z, x, 1 - c)
    to_right, to_left = at(z, right, c), at(z, left, c)
    z_peers = [at(mod4(z + d), x, c) for d in (1, 2, 3)]
    y_peers = [at_tp(zh, mod4(y + d)) for d in (1, 3)]
    opposite = at_tp(1 - zh, y)
    parity = lax.rem(y, 2)
    y_pair = at_tp(zh, y + 1 - 2 * parity)
    def buf(k):
        if k == 0:
            return wkv
        if k <= PAIRS:
            return wq.at[k - 1]
        return wo.at[k - 1 - PAIRS]

    kv_col = pl.multiple_of(lax.div(t, 2) * HEAD, HEAD)
    own = []
    for k in range(CHUNKS):
        dst = buf(k).at[0, x, c]
        if k == 0:
            copy_k = pltpu.make_async_copy(wk_hbm.at[:, pl.ds(kv_col, HEAD)], dst, ls.at[0])
            copy_v = pltpu.make_async_copy(wv_hbm.at[:, pl.ds(kv_col, HEAD)], dst, ls.at[0])
            pl.when(parity == 0)(copy_k.start)
            pl.when(parity == 1)(copy_v.start)
            own.append(copy_k)
            continue
        if k <= PAIRS:
            src = wq_hbm.at[:, pl.ds((k - 1) * PAIR, PAIR)]
        else:
            src = wo_hbm.at[:, pl.ds((k - 1 - PAIRS) * OUT_COLS, OUT_COLS)]
        copy = pltpu.make_async_copy(src, dst, ls.at[k])
        copy.start()
        own.append(copy)
    load_tok = []
    for slot in range(4):
        part = WIDTH // 4
        col = pl.multiple_of(mod4(z + slot) * part, part)
        copy = pltpu.make_async_copy(
            tok_hbm.at[:, pl.ds(col, part)], tok.at[:, pl.ds(slot * part, part)], ls.at[CHUNKS + slot]
        )
        copy.start()
        load_tok.append(copy)
    res_col = pl.multiple_of(t * (OUT_COLS * OUT_CHUNKS), OUT_COLS)
    load_res = pltpu.make_async_copy(
        tok_hbm.at[:, pl.ds(res_col, OUT_COLS * OUT_CHUNKS)], res, ls.at[CHUNKS + 4]
    )
    load_cos = pltpu.make_async_copy(cos_hbm, cosv, ls.at[CHUNKS + 5])
    load_sin = pltpu.make_async_copy(sin_hbm, sinv, ls.at[CHUNKS + 6])
    for copy in (load_res, load_cos, load_sin):
        copy.start()

    barrier = pltpu.get_barrier_semaphore()
    partners = [sibling, to_right, to_left, *z_peers, *y_peers, opposite]
    for partner in partners:
        pl.semaphore_signal(barrier, inc=1, device_id=partner, device_id_type=MESH)
    pl.semaphore_wait(barrier, len(partners))

    sent = []

    def send(src, dst, device):
        i = len(sent)
        copy = pltpu.make_async_remote_copy(
            src_ref=src, dst_ref=dst, send_sem=ss.at[i], recv_sem=rs.at[i],
            device_id=device, device_id_type=MESH,
        )
        copy.start()
        sent.append(copy)
        return copy

    along_z, own_x, rest_x, forwarded, across = {}, {}, {}, {}, {}

    def z_send(k):
        b = buf(k)
        mine = b.at[0, x, c]
        along_z[k] = [send(mine, b.at[4 - d, x, c], z_peers[d - 1]) for d in (1, 3, 2)]

    def own_send(k):
        mine = buf(k).at[0, x, c]
        own_x[k] = [send(mine, mine, to_right), send(mine, mine, to_left)]

    def rest_send(k):
        for copy in along_z[k]:
            copy.wait_recv()
        rest = buf(k).at[pl.ds(1, 3), x, c]
        rest_x[k] = [send(rest, rest, to_right), send(rest, rest, to_left)]
        column = buf(k).at[:, x, c]
        across[k] = [send(column, column, sibling)]

    def own_forward(k):
        own_x[k][0].wait_recv()
        block = buf(k).at[0, left, c]
        forwarded[k] = [send(block, block, to_right)]
        own_x[k][1].wait_recv()

    def rest_forward(k):
        rest_x[k][0].wait_recv()
        block = buf(k).at[1, left, c]
        forwarded[k].append(send(block, block, to_right))
        rest_x[k][1].wait_recv()
        block = buf(k).at[pl.ds(2, 2), right, c]
        forwarded[k].append(send(block, block, to_left))
        for side in (left, right):
            column = buf(k).at[:, side, c]
            across[k].append(send(column, column, sibling))

    def finish(k):
        for copy in forwarded[k]:
            copy.wait_recv()
        last = buf(k).at[:, far, c]
        across[k].append(send(last, last, sibling))
        for copy in across[k]:
            copy.wait_recv()

    def statistics():
        for copy in load_tok:
            copy.wait()

        @pl.loop(0, TOK // 32)
        def _(i):
            rows = pl.ds(pl.multiple_of(i * 32, 32), 32)
            wide = tok[rows, :].astype(jnp.float32)
            mean = jnp.sum(wide * wide, axis=1, keepdims=True) * (1.0 / WIDTH)
            scale[rows, :] = jnp.broadcast_to(lax.rsqrt(mean + 1e-6), (32, HEAD))

    def rotate(field, rows):
        return field * cosv[rows, :] + pltpu.roll(field, HEAD // 2, 1) * sinv[rows, :]

    def row_blocks(step):
        def run(work):
            @pl.loop(0, TOK // step)
            def _(i):
                work(pl.ds(pl.multiple_of(i * step, step), step))
        return run

    pair = []

    def key_or_value():
        for copy in (load_cos, load_sin):
            copy.wait()

        @row_blocks(ROWS)
        def _(rows):
            field = jnp.dot(
                tok[rows, :], wkv[...].reshape(WIDTH, HEAD), preferred_element_type=jnp.float32
            ) * scale[rows, :]
            kv[parity, rows, :] = jnp.where(parity == 0, rotate(field, rows), field).astype(jnp.bfloat16)

        pair.append(send(kv.at[parity], kv.at[parity], y_pair))

    def head_index(zh_, y_, p):
        owner = zh_ * 4 + y_
        slot = mod4(lax.div(owner, 2) - z + 4)
        return slot * 4 + lax.rem(owner, 2) * PAIRS + p

    near_heads, far_heads, last_heads = {}, {}, {}

    def attend(p):
        @row_blocks(ROWS)
        def _(rows):
            product = jnp.dot(
                tok[rows, :], wq[p].reshape(WIDTH, PAIR), preferred_element_type=jnp.float32
            )
            for h in range(2):
                cols = slice(h * HEAD, (h + 1) * HEAD)
                field = product[:, cols] * scale[rows, :]
                query[rows, cols] = rotate(field, rows).astype(jnp.bfloat16)

        if p == 0:
            pair[0].wait_recv()
        step = 256
        blocks = [(h, i) for h in range(2) for i in range(TOK // step)]
        scores = []
        for h, i in blocks:
            extent = (i + 1) * step
            score = lax.dot_general(
                query[i * step : extent, h * HEAD : (h + 1) * HEAD], kv[0, :extent, :],
                (((1,), (1,)), ((), ())), preferred_element_type=jnp.float32,
            ) * (HEAD ** -0.5)
            q_pos = lax.broadcasted_iota(jnp.int32, (step, extent), 0) + i * step
            k_pos = lax.broadcasted_iota(jnp.int32, (step, extent), 1)
            scores.append(jnp.where(q_pos >= k_pos, score, -1e30))
        parts = []
        for (h, i), score in zip(blocks, scores):
            expo = jnp.exp(score - jnp.max(score, axis=1, keepdims=True))
            norm = jnp.sum(expo, axis=1, keepdims=True)
            part = jnp.dot(
                expo.astype(jnp.bfloat16), kv[1, : (i + 1) * step, :],
                preferred_element_type=jnp.float32,
            )
            parts.append((part * (1.0 / norm)).astype(jnp.bfloat16))
        for (h, i), part in zip(blocks, parts):
            heads[head_index(zh, y, p), i * step : (i + 1) * step, h * HEAD : (h + 1) * HEAD] = part
        block = heads.at[head_index(zh, y, p)]
        near_heads[p] = [send(block, block, opposite)]

    def share(p):
        block = heads.at[head_index(zh, y, p)]
        near_heads[p] += [send(block, block, peer) for peer in y_peers]

    def relay_heads(p, near):
        pairs_of = (near_heads if near else far_heads)[p]
        first = 1 if near else 0
        side = zh if near else 1 - zh
        for i, (y_, device, half) in enumerate(((mod4(y + 3), y_peers[0], 0), (mod4(y + 1), y_peers[1], 1))):
            pairs_of[first + i].wait_recv()
            rows = pl.ds(half * (TOK // 2), TOK // 2)
            block = heads.at[head_index(side, y_, p), rows]
            last_heads.setdefault((p, near), []).append(send(block, block, device))

    def pass_on(p):
        near_heads[p][0].wait_recv()
        block = heads.at[head_index(1 - zh, y, p)]
        far_heads[p] = [send(block, block, peer) for peer in y_peers]

    def gather_heads(*keys):
        for key in keys:
            for copy in last_heads[key]:
                copy.wait_recv()

    stores = []

    def times(j, rows, indices):
        product = None
        for i in indices:
            block = wo[j, lax.div(i, 4), lax.rem(i, 4)].reshape(PAIR, OUT_COLS)
            term = jnp.dot(heads[i, rows, :], block, preferred_element_type=jnp.float32)
            product = term if product is None else product + term
        return product

    def output_most(j):
        cols = pl.ds(j * OUT_COLS, OUT_COLS)

        @row_blocks(ROWS)
        def _(rows):
            indices = [head_index(zh_, y_, 0) for zh_ in range(2) for y_ in range(4)]
            indices += [head_index(zh, y_, 1) for y_ in range(4)]
            total[rows, cols] = res[rows, cols].astype(jnp.float32) + times(j, rows, indices)

    def output(j):
        cols = pl.ds(j * OUT_COLS, OUT_COLS)

        @row_blocks(ROWS)
        def _(rows):
            indices = [head_index(1 - zh, y_, 1) for y_ in range(4)]
            outv[rows, cols] = (total[rows, cols] + times(j, rows, indices)).astype(jnp.bfloat16)

        store = pltpu.make_async_copy(outv.at[:, cols], out_hbm.at[:, cols], ls.at[CHUNKS + 7 + j])
        store.start()
        stores.append(store)

    own[0].wait()
    z_send(0)
    own_send(0)
    for k in range(1, CHUNKS):
        own[k].wait()
    own_send(1)
    own_send(2)
    rest_send(0)
    z_send(1)
    own_forward(0)
    own_send(3)
    own_forward(1)
    statistics()
    own_forward(2)
    rest_forward(0)
    own_send(4)
    rest_send(1)
    z_send(2)
    z_send(3)
    own_forward(3)
    finish(0)
    key_or_value()
    own_forward(4)
    own_send(5)
    rest_forward(1)
    rest_send(2)
    z_send(4)
    z_send(5)
    z_send(6)
    finish(1)
    attend(0)
    share(0)
    own_send(6)
    own_forward(5)
    rest_forward(2)
    rest_send(3)
    relay_heads(0, True)
    own_forward(6)
    finish(2)
    rest_send(4)
    attend(1)
    share(1)
    rest_forward(3)
    pass_on(0)
    rest_send(5)
    finish(3)
    rest_forward(4)
    rest_send(6)
    relay_heads(0, False)
    relay_heads(1, True)
    finish(4)
    pass_on(1)
    rest_forward(5)
    load_res.wait()
    finish(5)
    gather_heads((0, True), (0, False), (1, True))
    output_most(0)
    relay_heads(1, False)
    output_most(1)
    rest_forward(6)
    output_most(2)
    early = len(sent) - 16
    for copy in sent[:early]:
        copy.wait_send()
    gather_heads((1, False))
    output(0)
    output(1)
    output(2)
    finish(6)
    output_most(3)
    output(3)
    for copy in sent[early:]:
        copy.wait_send()
    for store in stores:
        store.wait()


def body(tokens, w_query, w_key, value_weight, w_out):
    cosine, sine = rotary_tables()
    any_space = pl.BlockSpec(memory_space=pl.ANY)
    blocks = (4, 4, 2)
    return pl.pallas_call(
        kernel,
        out_shape=jax.ShapeDtypeStruct((TOK, OUT_COLS * OUT_CHUNKS), jnp.bfloat16),
        in_specs=[any_space] * 7,
        out_specs=any_space,
        scratch_shapes=[
            pltpu.VMEM((TOK, WIDTH), jnp.bfloat16),
            pltpu.VMEM((*blocks, 256, HEAD), jnp.bfloat16),
            pltpu.VMEM((PAIRS, *blocks, 256, PAIR), jnp.bfloat16),
            pltpu.VMEM((OUT_CHUNKS, *blocks, 128, OUT_COLS), jnp.bfloat16),
            pltpu.VMEM((FEATURES // PAIR, TOK, PAIR), jnp.bfloat16),
            pltpu.VMEM((TOK, PAIR), jnp.bfloat16),
            pltpu.VMEM((2, TOK, HEAD), jnp.bfloat16),
            pltpu.VMEM((TOK, OUT_COLS * OUT_CHUNKS), jnp.bfloat16),
            pltpu.VMEM((TOK, HEAD), jnp.float32),
            pltpu.VMEM((TOK, HEAD), jnp.float32),
            pltpu.VMEM((TOK, OUT_COLS * OUT_CHUNKS), jnp.bfloat16),
            pltpu.VMEM((TOK, OUT_COLS * OUT_CHUNKS), jnp.float32),
            pltpu.VMEM((TOK, HEAD), jnp.float32),
            pltpu.SemaphoreType.DMA((SEMS,)),
            pltpu.SemaphoreType.DMA((SEMS,)),
            pltpu.SemaphoreType.DMA((CHUNKS + 7 + OUT_CHUNKS,)),
        ],
        compiler_params=pltpu.CompilerParams(
            collective_id=0, has_side_effects=True, vmem_limit_bytes=60 * 2**20
        ),
        cost_estimate=pl.CostEstimate(flops=11 * 10**9, bytes_accessed=12 * 2**20, transcendentals=2**20),
    )(tokens, w_query, w_key, value_weight, w_out, jnp.asarray(cosine), jnp.asarray(sine))


def solution(mesh):
    placed = (P("rep", None), P("rep", "tp"), P("rep", None), P("rep", None), P("rep", "tp"))
    return jax.shard_map(
        body, mesh=mesh, in_specs=placed, out_specs=P("rep", "tp"), check_vma=False
    )
```
